256 devices in a mesh: row: 16 (over x, z_hi, core), col: 16 (over z_lo, y).
Axes of the slice: x: 4, y: 4, z: 8 (z_hi: 2, z_lo: 4; z = z_hi * 4 + z_lo), core: 2. Of those that a mesh axis runs over, the one named last changes fastest.
Arguments:
- inputs: bfloat16 [512, 12288], P('col', 'row'), may hold values from -6 to 6
- w_up: bfloat16 [12288, 24576], P('row', 'col'), may hold values from -0.0546875 to 0.0546875
- w_down: bfloat16 [24576, 12288], P('col', 'row'), may hold values from -0.0390625 to 0.0390625
- grad_out: bfloat16 [512, 12288], P('col', 'row'), may hold values from -1.5 to 1.5
Outputs:
- outputs: bfloat16 [512, 12288], P('col', 'row')
- grad_in: bfloat16 [512, 12288], P('col', 'row')
- grad_up: bfloat16 [12288, 24576], P('row', 'col')
- grad_down: bfloat16 [24576, 12288], P('col', 'row')
The draws below stay inside these ranges and needn't reach their ends.
All inputs are finite; a program needn't handle non-finite values.
Results may differ from the reference program's by a relative error of at most 0.005.
Values may be sent and summed in bfloat16 or wider, within the bound.
A program may use at most 64 MiB of HBM per device.

```python
import jax
import jax.numpy as jnp

D = 12288
FF = 24576
TOKENS = 512


def shard_levels(key, extent, split, smallest, top_value):
    def one(dim, shards_of):
        steps = jax.random.uniform(jax.random.fold_in(jax.random.fold_in(key, 6), dim), (shards_of,), jnp.float32, smallest / len(split), top_value / len(split))
        return jnp.repeat(jnp.exp(steps), extent[dim] // shards_of).reshape((-1,) + (1,) * (len(extent) - dim - 1))

    factor_of = one(*split[0])
    for cut in split[1:]:
        factor_of = factor_of * one(*cut)
    return factor_of


def noise(own_key, dims, scale, most, shards=(), kind=jnp.bfloat16):
    entries = jax.random.normal(own_key, dims, jnp.float32) * scale
    if len(shards) > 0:
        entries = shard_levels(own_key, dims, shards, -0.22, 0.18) * entries
    return jnp.clip(entries, min=-most, max=most).astype(kind)


def setup_inputs(seed: int = 0) -> dict:
    seeds = jax.random.split(jax.random.key(seed), 5)
    return {
        "inputs": noise(seeds[0], (TOKENS, D), 1.0, 6.0, ((0, 16), (1, 16))),
        "w_up": noise(seeds[1], (D, FF), D ** -0.5, 0.0546875, ((0, 16), (1, 16))),
        "w_down": noise(seeds[2], (FF, D), FF ** -0.5, 0.0390625, ((0, 16), (1, 16))),
        "grad_out": noise(seeds[3], (TOKENS, D), 0.25, 1.5, ((0, 16), (1, 16))),
    }


def gelu_tanh(value):
    inner = 0.7978845608 * (value + 0.044715 * value * value * value)
    return 0.5 * value * (1.0 + jnp.tanh(inner))

def reference(inputs, w_up, w_down, grad_out):
    hidden = jnp.dot(inputs, w_up, preferred_element_type=jnp.float32)
    active, pullback = jax.vjp(gelu_tanh, hidden)
    active = active.astype(jnp.bfloat16)
    outputs = jnp.dot(active, w_down, preferred_element_type=jnp.float32).astype(jnp.bfloat16)
    grad_active = jnp.dot(grad_out, w_down.T, preferred_element_type=jnp.float32)
    grad_hidden = pullback(grad_active)[0].astype(jnp.bfloat16)
    grad_down = jnp.dot(active.T, grad_out, preferred_element_type=jnp.float32).astype(jnp.bfloat16)
    grad_up = jnp.dot(inputs.T, grad_hidden, preferred_element_type=jnp.float32).astype(jnp.bfloat16)
    grad_in = jnp.dot(grad_hidden, w_up.T, preferred_element_type=jnp.float32).astype(jnp.bfloat16)
    return (outputs, grad_in, grad_up, grad_down)
```

```python
import functools

import jax
import jax.numpy as jnp
from jax import lax
from jax.experimental import pallas as pl
from jax.experimental.pallas import tpu as pltpu
from jax.sharding import PartitionSpec as P

MESH = pl.DeviceIdType.MESH
BF16, F32 = jnp.bfloat16, jnp.float32
ORDER = (
    (0, 1, 0), (1, 0, 0), (0, 1, 1), (1, 0, 1), (2, 0, 0), (0, 2, 0), (0, 2, 1), (1, 1, 0),
    (2, 0, 1), (0, 3, 0), (1, 1, 1), (2, 1, 0), (0, 3, 1), (3, 0, 0), (1, 2, 0), (2, 1, 1),
    (1, 2, 1), (3, 0, 1), (2, 2, 0), (1, 3, 0), (3, 1, 0), (2, 2, 1), (4, 0, 0), (1, 3, 1),
    (3, 1, 1), (2, 3, 0), (4, 0, 1), (3, 2, 0), (2, 3, 1), (4, 1, 0), (3, 2, 1), (5, 0, 0),
    (4, 1, 1), (3, 3, 0), (5, 0, 1), (3, 3, 1), (4, 2, 0), (5, 1, 0), (6, 0, 0), (4, 2, 1),
    (5, 1, 1), (7, 0, 0), (6, 0, 1), (4, 3, 0), (4, 3, 1), (6, 1, 0), (5, 2, 0), (7, 0, 1),
    (5, 2, 1), (7, 1, 0), (6, 1, 1), (8, 0, 0), (5, 3, 0), (7, 1, 1), (6, 2, 0), (5, 3, 1),
    (8, 0, 1), (6, 2, 1), (7, 2, 0), (8, 1, 0), (7, 2, 1), (6, 3, 0), (8, 1, 1), (6, 3, 1),
    (7, 3, 0), (7, 3, 1), (8, 2, 0), (8, 2, 1), (8, 3, 0), (8, 3, 1),
)


def tanh_of(value):
    return jnp.tanh(0.7978845608 * (value + 0.044715 * value * value * value))


def gelu(value):
    return 0.5 * value * (1.0 + tanh_of(value))


def gelu_slope(value):
    t = tanh_of(value)
    inner_slope = 0.7978845608 * (1.0 + 3.0 * 0.044715 * value * value)
    return 0.5 * (1.0 + t) + 0.5 * value * (1.0 - t * t) * inner_slope


def contract(left, right, left_dim, right_dim):
    return lax.dot_general(
        left, right, (((left_dim,), (right_dim,)), ((), ())), preferred_element_type=F32
    )


def at(start, size):
    return pl.ds(pl.multiple_of(start, size), size)


def kernel(
    inputs, w_up, w_down, grad_out, outputs, grad_in, grad_up, grad_down,
    tokens, up, down, act, up_out, down_out,
    core_out, core_in, mine, x_out, x_in, sums, zh_out, zh_in, hidden,
    part, y_out, y_in, kept, z_out, z_in,
    load_sem, store_sem, own_sem, sent, got,
):
    row, col = lax.axis_index("row"), lax.axis_index("col")
    x, zh, core = row // 4, (row // 2) % 2, row % 2
    zl, y = col // 4, col % 4
    other_core = (row + 1 - 2 * core, col)
    partner = (row + 2 - 4 * zh, col)
    xs = [((row + 4 * d) % 16, col) for d in (1, 2, 3)]
    ys = [(row, zl * 4 + (y + d) % 4) for d in (1, 2, 3)]
    planes = [zl, zl + 1 - 2 * (zl % 2), (zl + 2) % 4, 3 - zl]
    zs = [(row, plane * 4 + y) for plane in planes[1:]]
    shards = (inputs, grad_out)

    loads = []
    for half in range(2):
        for k, (src, dst) in enumerate((
            (w_up.at[:, pl.ds(half * 768, 768)], up.at[half]),
            (w_down.at[pl.ds(half * 768, 768)], down.at[half]),
        )):
            loads.append(pltpu.make_async_copy(src, dst, load_sem.at[k, half]))
    own = [
        pltpu.make_async_copy(shards[a], tokens.at[a, at(y * 32, 32)], own_sem.at[a])
        for a in range(2)
    ]
    for copy in own + loads:
        copy.start()

    barrier = pltpu.get_barrier_semaphore()
    everyone = [other_core, partner] + xs + ys + zs
    for device in everyone:
        pl.semaphore_signal(barrier, inc=1, device_id=device, device_id_type=MESH)
    pl.semaphore_wait(barrier, len(everyone))

    flights = {}

    def send(src, dst, device, send_sem, recv_sem, rows):
        pltpu.make_async_remote_copy(
            src_ref=src, dst_ref=dst, send_sem=sent.at[send_sem], recv_sem=got.at[recv_sem],
            device_id=device, device_id_type=MESH,
        ).start()
        flights[send_sem] = flights.get(send_sem, 0) + rows

    def arrived(ref, recv_sem):
        pltpu.make_async_copy(ref, ref, got.at[recv_sem]).wait()

    def sem(step, q):
        return 8 + 8 * step + q

    for a in range(2):
        here = tokens.at[a, at(y * 32, 32)]
        for device in ys:
            send(shards[a], here, device, a, a, 32)
    for j in (1, 2, 3):
        for a in range(2):
            there = tokens.at[a, at(j * 128 + y * 32, 32)]
            send(shards[a], there, zs[j - 1], sem(0, 2 * j + a), sem(0, 2 * j + a), 32)

    weights_here = set()

    def weights(k):
        if k not in weights_here:
            weights_here.add(k)
            for half in range(2):
                loads[2 * half + k].wait()

    for step, j, a in ORDER:
        q = 2 * j + a
        chunk = pl.ds(j * 128, 128)
        group = at(j * 128 + x * 32, 32)
        piece = at(j * 128 + x * 32 + zh * 16, 16)
        if step == 0:
            shard = tokens.at[a, at(j * 128 + y * 32, 32)]
            arrived(shard, sem(0, q))
            for device in ys:
                send(shard, shard, device, q, q, 32)
        elif step == 1:
            if j == 0:
                own[a].wait()
                weights(a)
            arrived(tokens.at[a, pl.ds(j * 128, 96)], q)
            block = tokens[a, chunk]

            def product(half):
                if a == 0:
                    return contract(block, up[half], 1, 0)
                return contract(block, down[half], 1, 1)

            core_out[q] = product(1 - core)
            send(core_out.at[q], core_in.at[q], other_core, sem(1, q), sem(1, q), 256)
            mine[q] = product(core)
        elif step == 2:
            arrived(core_in.at[q], sem(1, q))
            both = mine[q] + core_in[q]
            mine[q] = both
            x_out[q] = both.astype(BF16)
            for d in (1, 2, 3):
                theirs = x_out.at[q, at((x + d) % 4 * 32, 32)]
                send(theirs, x_in.at[q, d - 1], xs[d - 1], sem(2, q), sem(2, q), 32)
        elif step == 3:
            arrived(x_in.at[q], sem(2, q))
            total = mine[q, at(x * 32, 32)]
            for d in range(3):
                total = total + x_in[q, d].astype(F32)
            sums[q] = total
            zh_out[q] = total.astype(BF16)
            send(zh_out.at[q, at((1 - zh) * 16, 16)], zh_in.at[q], partner, sem(3, q), sem(3, q), 16)
        elif step == 4:
            arrived(zh_in.at[q], sem(3, q))
            total = sums[q, at(zh * 16, 16)] + zh_in[q].astype(F32)
            if a == 0:
                hidden[j] = total
                result = gelu(total)
            else:
                result = total * gelu_slope(hidden[j])
            act[a, core, piece] = result.astype(BF16)
            theirs = act.at[a, core, piece]
            send(theirs, theirs, partner, sem(4, q), sem(4, q), 16)
        elif step == 5:
            arrived(zh_in.at[q], sem(4, q))
            theirs = act.at[a, core, group]
            for device in xs:
                send(theirs, theirs, device, sem(5, q), sem(5, q), 32)
        elif step == 6:
            arrived(act.at[a, core, pl.ds(j * 128, 96)], sem(5, q))
            theirs = act.at[a, core, chunk]
            send(theirs, theirs, other_core, sem(6, q), sem(6, q), 128)
        elif step == 7:
            def term(half):
                block = act[a, half, chunk]
                if a == 0:
                    return contract(block, down[half], 1, 0)
                return contract(block, up[half], 1, 1)

            total = term(core)
            arrived(act.at[a, 1 - core, chunk], sem(6, q))
            total = total + term(1 - core)
            part[q] = total
            y_out[q] = total.astype(BF16)
            for d in (1, 2, 3):
                theirs = y_out.at[q, at((y + d) % 4 * 32, 32)]
                send(theirs, y_in.at[q, d - 1], ys[d - 1], sem(7, q), sem(7, q), 32)
        else:
            arrived(y_in.at[q], sem(7, q))
            total = part[q, at(y * 32, 32)]
            for d in range(3):
                total = total + y_in[q, d].astype(F32)
            if j == 0:
                kept[a] = total
            else:
                z_out[a, j - 1] = total.astype(BF16)
                send(z_out.at[a, j - 1], z_in.at[a, j - 1], zs[j - 1], sem(8, a), sem(8, a), 32)
        if (step, j) == (7, 3):
            for half in range(2):
                if a == 0:
                    down_out[half] = contract(act[0, half], tokens[1], 0, 0).astype(BF16)
                    src, dst = down_out.at[half], grad_down.at[pl.ds(half * 768, 768)]
                else:
                    up_out[half] = contract(tokens[0], act[1, half], 0, 0).astype(BF16)
                    src, dst = up_out.at[half], grad_up.at[:, pl.ds(half * 768, 768)]
                pltpu.make_async_copy(src, dst, store_sem.at[a, half]).start()

    for a, result in enumerate((outputs, grad_in)):
        arrived(z_in.at[a], sem(8, a))
        total = kept[a]
        for j in range(3):
            total = total + z_in[a, j].astype(F32)
        result[...] = total.astype(BF16)

    for half in range(2):
        pltpu.make_async_copy(
            down_out.at[half], grad_down.at[pl.ds(half * 768, 768)], store_sem.at[0, half]
        ).wait()
        pltpu.make_async_copy(
            up_out.at[half], grad_up.at[:, pl.ds(half * 768, 768)], store_sem.at[1, half]
        ).wait()
    for send_sem, rows in flights.items():
        ref = tokens.at[0, pl.ds(0, rows)]
        pltpu.make_async_copy(ref, ref, sent.at[send_sem]).wait()


def on_device(inputs, w_up, w_down, grad_out):
    shape = jax.ShapeDtypeStruct
    hbm, vmem = pl.BlockSpec(memory_space=pl.ANY), pl.BlockSpec(memory_space=pltpu.VMEM)
    return pl.pallas_call(
        kernel,
        out_shape=(
            shape((32, 768), BF16), shape((32, 768), BF16),
            shape((768, 1536), BF16), shape((1536, 768), BF16),
        ),
        in_specs=[hbm] * 4,
        out_specs=(vmem, vmem, hbm, hbm),
        scratch_shapes=[
            pltpu.VMEM((2, 512, 768), BF16),
            pltpu.VMEM((2, 768, 768), BF16),
            pltpu.VMEM((2, 768, 768), BF16),
            pltpu.VMEM((2, 2, 512, 768), BF16),
            pltpu.VMEM((2, 768, 768), BF16),
            pltpu.VMEM((2, 768, 768), BF16),
            pltpu.VMEM((8, 128, 768), F32),
            pltpu.VMEM((8, 128, 768), F32),
            pltpu.VMEM((8, 128, 768), F32),
            pltpu.VMEM((8, 128, 768), BF16),
            pltpu.VMEM((8, 3, 32, 768), BF16),
            pltpu.VMEM((8, 32, 768), F32),
            pltpu.VMEM((8, 32, 768), BF16),
            pltpu.VMEM((8, 16, 768), BF16),
            pltpu.VMEM((4, 16, 768), F32),
            pltpu.VMEM((8, 128, 768), F32),
            pltpu.VMEM((8, 128, 768), BF16),
            pltpu.VMEM((8, 3, 32, 768), BF16),
            pltpu.VMEM((2, 32, 768), F32),
            pltpu.VMEM((2, 3, 32, 768), BF16),
            pltpu.VMEM((2, 3, 32, 768), BF16),
            pltpu.SemaphoreType.DMA((2, 2)),
            pltpu.SemaphoreType.DMA((2, 2)),
            pltpu.SemaphoreType.DMA((2,)),
            pltpu.SemaphoreType.DMA((80,)),
            pltpu.SemaphoreType.DMA((80,)),
        ],
        compiler_params=pltpu.CompilerParams(
            collective_id=0, has_side_effects=True, vmem_limit_bytes=56 << 20
        ),
    )(inputs, w_up, w_down, grad_out)


def solution(mesh):
    placed = (P("col", "row"), P("row", "col"), P("col", "row"), P("col", "row"))
    return jax.shard_map(
        on_device,
        mesh=mesh,
        in_specs=placed,
        out_specs=(P("col", "row"), P("col", "row"), P("row", "col"), P("col", "row")),
        check_vma=False,
    )
```

```python
import functools

import jax
import jax.numpy as jnp
from jax import lax
from jax.experimental import pallas as pl
from jax.experimental.pallas import tpu as pltpu
from jax.sharding import PartitionSpec as P

MESH = pl.DeviceIdType.MESH
BF16, F32 = jnp.bfloat16, jnp.float32
ORDER = (
    (1, 0, 0), (0, 3, 0), (2, 0, 0), (0, 3, 1), (0, 2, 0), (0, 2, 1), (0, 1, 0), (1, 3, 0),
    (0, 1, 1), (0, 0, 1), (3, 0, 0), (1, 3, 1), (2, 3, 0), (1, 2, 0), (2, 3, 1), (1, 2, 1),
    (2, 2, 0), (1, 1, 0), (4, 0, 0), (3, 3, 0), (2, 2, 1), (1, 1, 1), (3, 3, 1), (2, 1, 0),
    (1, 0, 1), (3, 2, 0), (2, 1, 1), (2, 0, 1), (6, 0, 0), (4, 3, 0), (3, 2, 1), (7, 0, 0),
    (4, 3, 1), (3, 1, 0), (4, 2, 0), (3, 1, 1), (3, 0, 1), (4, 2, 1), (8, 0, 0), (6, 3, 0),
    (4, 1, 0), (7, 3, 0), (6, 3, 1), (4, 1, 1), (6, 2, 0), (4, 0, 1), (7, 3, 1), (6, 2, 1),
    (7, 2, 0), (6, 1, 0), (7, 2, 1), (8, 3, 0), (6, 1, 1), (7, 1, 0), (7, 1, 1), (8, 3, 1),
    (6, 0, 1), (8, 2, 0), (7, 0, 1), (8, 2, 1), (8, 1, 0), (8, 1, 1), (8, 0, 1),
)


def tanh_of(value):
    return jnp.tanh(0.7978845608 * (value + 0.044715 * value * value * value))


def gelu(value):
    return 0.5 * value * (1.0 + tanh_of(value))


def gelu_slope(value):
    t = tanh_of(value)
    inner_slope = 0.7978845608 * (1.0 + 3.0 * 0.044715 * value * value)
    return 0.5 * (1.0 + t) + 0.5 * value * (1.0 - t * t) * inner_slope


def contract(left, right, left_dim, right_dim):
    return lax.dot_general(
        left, right, (((left_dim,), (right_dim,)), ((), ())), preferred_element_type=F32
    )


def at(start, size):
    return pl.ds(pl.multiple_of(start, size), size)


def kernel(
    inputs, w_up, w_down, grad_out, outputs, grad_in, grad_up, grad_down,
    tokens, up, down, act,
    core_out, core_in, mine, x_out, x_in, sums, zh_out, zh_in, hidden,
    part, y_out, y_in, kept, z_out, z_in,
    load_sem, own_sem, sent, got,
):
    row, col = lax.axis_index("row"), lax.axis_index("col")
    x, zh, core = row // 4, (row // 2) % 2, row % 2
    zl, y = col // 4, col % 4
    other_core = (row + 1 - 2 * core, col)
    partner = (row + 2 - 4 * zh, col)
    xs = [((row + 4 * d) % 16, col) for d in (1, 2, 3)]
    ys = [(row, zl * 4 + (y + d) % 4) for d in (1, 2, 3)]
    planes = [zl, zl + 1 - 2 * (zl % 2), (zl + 2) % 4, 3 - zl]
    zs = [(row, plane * 4 + y) for plane in planes[1:]]
    shards = (inputs, grad_out)

    loads = []
    for half in range(2):
        for k, (src, dst) in enumerate((
            (w_up.at[:, pl.ds(half * 768, 768)], up.at[half]),
            (w_down.at[pl.ds(half * 768, 768)], down.at[half]),
        )):
            loads.append(pltpu.make_async_copy(src, dst, load_sem.at[k, half]))
    own = [
        pltpu.make_async_copy(shards[a], tokens.at[a, at(y * 32, 32)], own_sem.at[a])
        for a in range(2)
    ]
    for copy in own + loads:
        copy.start()

    barrier = pltpu.get_barrier_semaphore()
    everyone = [other_core, partner] + xs + ys + zs
    for device in everyone:
        pl.semaphore_signal(barrier, inc=1, device_id=device, device_id_type=MESH)
    pl.semaphore_wait(barrier, len(everyone))

    flights = {}

    def send(src, dst, device, send_sem, recv_sem, rows):
        pltpu.make_async_remote_copy(
            src_ref=src, dst_ref=dst, send_sem=sent.at[send_sem], recv_sem=got.at[recv_sem],
            device_id=device, device_id_type=MESH,
        ).start()
        flights[send_sem] = flights.get(send_sem, 0) + rows

    def arrived(ref, recv_sem):
        pltpu.make_async_copy(ref, ref, got.at[recv_sem]).wait()

    def sem(step, q):
        return 8 + 8 * step + q

    def share(a):
        here = tokens.at[a, at(y * 32, 32)]
        for device in ys:
            send(shards[a], here, device, a, a, 32)

    share(0)
    for j in (3, 2, 1):
        for a in range(2):
            there = tokens.at[a, at(j * 128 + y * 32, 32)]
            send(shards[a], there, zs[j - 1], sem(0, 2 * j + a), sem(0, 2 * j + a), 32)

    weights_here = set()

    def weights(k):
        if k not in weights_here:
            weights_here.add(k)
            for half in range(2):
                loads[2 * half + k].wait()

    for step, j, a in ORDER:
        q = 2 * j + a
        chunk = pl.ds(j * 128, 128)
        group = at(j * 128 + x * 32, 32)
        if step == 0 and j == 0:
            share(a)
        elif step == 0:
            shard = tokens.at[a, at(j * 128 + y * 32, 32)]
            arrived(shard, sem(0, q))
            for device in ys:
                send(shard, shard, device, q, q, 32)
        elif step == 1:
            if j == 0:
                own[a].wait()
            weights(a)
            arrived(tokens.at[a, pl.ds(j * 128, 96)], q)
            block = tokens[a, chunk]

            def product(half):
                if a == 0:
                    return contract(block, up[half], 1, 0)
                return contract(block, down[half], 1, 1)

            core_out[q] = product(1 - core)
            send(core_out.at[q], core_in.at[q], other_core, sem(1, q), sem(1, q), 256)
            mine[q] = product(core)
        elif step == 2:
            arrived(core_in.at[q], sem(1, q))
            both = mine[q] + core_in[q]
            x_out[q] = both.astype(BF16)
            for d in (1, 2, 3):
                theirs = x_out.at[q, at((x + d) % 4 * 32, 32)]
                send(theirs, x_in.at[q, d - 1], xs[d - 1], sem(2, q), sem(2, q), 32)
        elif step == 3:
            arrived(x_in.at[q], sem(2, q))
            rows = at(x * 32, 32)
            total = mine[q, rows] + core_in[q, rows]
            for d in range(3):
                total = total + x_in[q, d].astype(F32)
            sums[q] = total
            zh_out[q] = total.astype(BF16)
            send(zh_out.at[q], zh_in.at[q], partner, sem(3, q), sem(3, q), 32)
        elif step == 4:
            arrived(zh_in.at[q], sem(3, q))
            total = sums[q] + zh_in[q].astype(F32)
            if a == 0:
                hidden[j] = total
                result = gelu(total)
            else:
                result = total * gelu_slope(hidden[j])
            act[a, core, group] = result.astype(BF16)
            theirs = act.at[a, core, group]
            for device in xs:
                send(theirs, theirs, device, sem(5, q), sem(5, q), 32)
        elif step == 6:
            arrived(act.at[a, core, pl.ds(j * 128, 96)], sem(5, q))
            theirs = act.at[a, core, chunk]
            send(theirs, theirs, other_core, sem(6, q), sem(6, q), 128)
        elif step == 7:
            weights(1 - a)

            def term(half):
                block = act[a, half, chunk]
                if a == 0:
                    return contract(block, down[half], 1, 0)
                return contract(block, up[half], 1, 1)

            total = term(core)
            arrived(act.at[a, 1 - core, chunk], sem(6, q))
            total = total + term(1 - core)
            part[q] = total
            y_out[q] = total.astype(BF16)
            for d in (1, 2, 3):
                theirs = y_out.at[q, at((y + d) % 4 * 32, 32)]
                send(theirs, y_in.at[q, d - 1], ys[d - 1], sem(7, q), sem(7, q), 32)
        else:
            arrived(y_in.at[q], sem(7, q))
            total = part[q, at(y * 32, 32)]
            for d in range(3):
                total = total + y_in[q, d].astype(F32)
            if j == 0:
                kept[a] = total
            else:
                z_out[a, j - 1] = total.astype(BF16)
                send(z_out.at[a, j - 1], z_in.at[a, j - 1], zs[j - 1], sem(8, a), sem(8, a), 32)

    for half in range(2):
        grad_down[pl.ds(half * 768, 768)] = contract(act[0, half], tokens[1], 0, 0).astype(BF16)
        grad_up[:, pl.ds(half * 768, 768)] = contract(tokens[0], act[1, half], 0, 0).astype(BF16)

    for a, result in enumerate((outputs, grad_in)):
        arrived(z_in.at[a], sem(8, a))
        total = kept[a]
        for j in range(3):
            total = total + z_in[a, j].astype(F32)
        result[...] = total.astype(BF16)

    for send_sem, rows in flights.items():
        ref = tokens.at[0, pl.ds(0, rows)]
        pltpu.make_async_copy(ref, ref, sent.at[send_sem]).wait()


def write(*refs):
    count = len(refs) // 2
    sem = refs[-1]
    copies = [
        pltpu.make_async_copy(refs[k], refs[count + k], sem.at[k]) for k in range(count)
    ]
    for copy in copies:
        copy.start()
    for copy in copies:
        copy.wait()


def on_device(inputs, w_up, w_down, grad_out):
    shapes = ((32, 768), (32, 768), (768, 1536), (1536, 768))
    hbm, vmem = pl.BlockSpec(memory_space=pltpu.HBM), pl.BlockSpec(memory_space=pltpu.VMEM)
    results = pl.pallas_call(
        kernel,
        out_shape=tuple(pltpu.VMEM(shape, BF16) for shape in shapes),
        in_specs=[hbm] * 4,
        out_specs=(vmem,) * 4,
        scratch_shapes=[
            pltpu.VMEM((2, 512, 768), BF16),
            pltpu.VMEM((2, 768, 768), BF16),
            pltpu.VMEM((2, 768, 768), BF16),
            pltpu.VMEM((2, 2, 512, 768), BF16),
            pltpu.VMEM((8, 128, 768), F32),
            pltpu.VMEM((8, 128, 768), F32),
            pltpu.VMEM((8, 128, 768), F32),
            pltpu.VMEM((8, 128, 768), BF16),
            pltpu.VMEM((8, 3, 32, 768), BF16),
            pltpu.VMEM((8, 32, 768), F32),
            pltpu.VMEM((8, 32, 768), BF16),
            pltpu.VMEM((8, 32, 768), BF16),
            pltpu.VMEM((4, 32, 768), F32),
            pltpu.VMEM((8, 128, 768), F32),
            pltpu.VMEM((8, 128, 768), BF16),
            pltpu.VMEM((8, 3, 32, 768), BF16),
            pltpu.VMEM((2, 32, 768), F32),
            pltpu.VMEM((2, 3, 32, 768), BF16),
            pltpu.VMEM((2, 3, 32, 768), BF16),
            pltpu.SemaphoreType.DMA((2, 2)),
            pltpu.SemaphoreType.DMA((2,)),
            pltpu.SemaphoreType.DMA((80,)),
            pltpu.SemaphoreType.DMA((80,)),
        ],
        compiler_params=pltpu.CompilerParams(
            collective_id=0, has_side_effects=True, vmem_limit_bytes=56 << 20
        ),
    )(inputs, w_up, w_down, grad_out)
    return pl.pallas_call(
        write,
        out_shape=tuple(jax.ShapeDtypeStruct(shape, BF16) for shape in shapes),
        in_specs=[pl.BlockSpec(memory_space=pl.ANY)] * 4,
        out_specs=(hbm,) * 4,
        scratch_shapes=[pltpu.SemaphoreType.DMA((4,))],
        compiler_params=pltpu.CompilerParams(vmem_limit_bytes=1 << 20),
    )(*results)


def solution(mesh):
    placed = (P("col", "row"), P("row", "col"), P("col", "row"), P("col", "row"))
    return jax.shard_map(
        on_device,
        mesh=mesh,
        in_specs=placed,
        out_specs=(P("col", "row"), P("col", "row"), P("row", "col"), P("col", "row")),
        check_vma=False,
    )
```

```python
import functools

import jax
import jax.numpy as jnp
from jax import lax
from jax.experimental import pallas as pl
from jax.experimental.pallas import tpu as pltpu
from jax.sharding import PartitionSpec as P

MESH = pl.DeviceIdType.MESH
BF16, F32 = jnp.bfloat16, jnp.float32
ORDER = (
    (0, 0, 1), (0, 1, 0), (1, 0, 0), (0, 2, 0), (1, 0, 1), (0, 3, 0), (2, 0, 0), (1, 1, 0),
    (0, 3, 1), (2, 0, 1), (1, 2, 0), (0, 2, 1), (2, 1, 0), (0, 1, 1), (1, 3, 0), (2, 2, 0),
    (1, 3, 1), (3, 0, 0), (2, 3, 0), (1, 2, 1), (3, 1, 0), (2, 3, 1), (1, 1, 1), (3, 2, 0),
    (2, 2, 1), (3, 3, 0), (2, 1, 1), (3, 3, 1), (4, 1, 0), (3, 2, 1), (4, 2, 0), (3, 1, 1),
    (4, 3, 0), (3, 0, 1), (4, 3, 1), (6, 1, 0), (4, 2, 1), (6, 2, 0), (7, 1, 0), (4, 1, 1),
    (6, 3, 0), (4, 0, 0), (7, 2, 0), (6, 3, 1), (7, 3, 0), (4, 0, 1), (6, 2, 1), (7, 3, 1),
    (6, 1, 1), (8, 1, 0), (7, 2, 1), (8, 2, 0), (6, 0, 0), (7, 1, 1), (8, 3, 0), (6, 0, 1),
    (7, 0, 0), (8, 3, 1), (7, 0, 1), (8, 2, 1), (8, 1, 1), (8, 0, 0), (8, 0, 1),
)


def tanh_of(value):
    return jnp.tanh(0.7978845608 * (value + 0.044715 * value * value * value))


def gelu(value):
    return 0.5 * value * (1.0 + tanh_of(value))


def gelu_slope(value):
    t = tanh_of(value)
    inner_slope = 0.7978845608 * (1.0 + 3.0 * 0.044715 * value * value)
    return 0.5 * (1.0 + t) + 0.5 * value * (1.0 - t * t) * inner_slope


def contract(left, right, left_dim, right_dim):
    return lax.dot_general(
        left, right, (((left_dim,), (right_dim,)), ((), ())), preferred_element_type=F32
    )


def at(start, size):
    return pl.ds(pl.multiple_of(start, size), size)


def kernel(
    inputs, w_up, w_down, grad_out, outputs, grad_in, grad_up, grad_down,
    tokens, up, down, act,
    core_out, core_in, mine, x_out, x_in, sums, zh_out, zh_in, hidden,
    part, y_out, y_in, kept, z_out, z_in,
    load_sem, own_sem, sent, got,
):
    row, col = lax.axis_index("row"), lax.axis_index("col")
    x, zh, core = row // 4, (row // 2) % 2, row % 2
    zl, y = col // 4, col % 4
    other_core = (row + 1 - 2 * core, col)
    partner = (row + 2 - 4 * zh, col)
    xs = [((row + 4 * d) % 16, col) for d in (1, 2, 3)]
    ys = [(row, zl * 4 + (y + d) % 4) for d in (1, 2, 3)]
    planes = [zl, zl + 1 - 2 * (zl % 2), (zl + 2) % 4, 3 - zl]
    zs = [(row, plane * 4 + y) for plane in planes[1:]]
    shards = (inputs, grad_out)

    loads = []
    for half in range(2):
        for k, (src, dst) in enumerate((
            (w_up.at[:, pl.ds(half * 768, 768)], up.at[half]),
            (w_down.at[pl.ds(half * 768, 768)], down.at[half]),
        )):
            loads.append(pltpu.make_async_copy(src, dst, load_sem.at[k, half]))
    own = [
        pltpu.make_async_copy(shards[a], tokens.at[a, at(y * 32, 32)], own_sem.at[a])
        for a in range(2)
    ]
    for copy in own + loads:
        copy.start()

    barrier = pltpu.get_barrier_semaphore()
    everyone = [other_core, partner] + xs + ys + zs
    for device in everyone:
        pl.semaphore_signal(barrier, inc=1, device_id=device, device_id_type=MESH)
    pl.semaphore_wait(barrier, len(everyone))

    flights = {}

    def send(src, dst, device, send_sem, recv_sem, rows):
        pltpu.make_async_remote_copy(
            src_ref=src, dst_ref=dst, send_sem=sent.at[send_sem], recv_sem=got.at[recv_sem],
            device_id=device, device_id_type=MESH,
        ).start()
        flights[send_sem] = flights.get(send_sem, 0) + rows

    def arrived(ref, recv_sem):
        pltpu.make_async_copy(ref, ref, got.at[recv_sem]).wait()

    def sem(step, q):
        return 8 + 8 * step + q

    def share(a):
        here = tokens.at[a, at(y * 32, 32)]
        for device in ys:
            send(shards[a], here, device, a, a, 32)

    share(0)
    for j, a in ((1, 0), (2, 0), (3, 0), (3, 1), (2, 1), (1, 1)):
        there = tokens.at[a, at(j * 128 + y * 32, 32)]
        send(shards[a], there, zs[j - 1], sem(0, 2 * j + a), sem(0, 2 * j + a), 32)

    weights_here = set()

    def weights(k):
        if k not in weights_here:
            weights_here.add(k)
            for half in range(2):
                loads[2 * half + k].wait()

    for step, j, a in ORDER:
        q = 2 * j + a
        chunk = pl.ds(j * 128, 128)
        group = at(j * 128 + x * 32, 32)
        if step == 0 and j == 0:
            share(a)
        elif step == 0:
            shard = tokens.at[a, at(j * 128 + y * 32, 32)]
            arrived(shard, sem(0, q))
            for device in ys:
                send(shard, shard, device, q, q, 32)
        elif step == 1:
            if j == 0:
                own[a].wait()
            weights(a)
            arrived(tokens.at[a, pl.ds(j * 128, 96)], q)
            block = tokens[a, chunk]

            def product(half):
                if a == 0:
                    return contract(block, up[half], 1, 0)
                return contract(block, down[half], 1, 1)

            core_out[q] = product(1 - core)
            send(core_out.at[q], core_in.at[q], other_core, sem(1, q), sem(1, q), 256)
            mine[q] = product(core)
        elif step == 2:
            arrived(core_in.at[q], sem(1, q))
            both = mine[q] + core_in[q]
            x_out[q] = both.astype(BF16)
            for d in (1, 2, 3):
                theirs = x_out.at[q, at((x + d) % 4 * 32, 32)]
                send(theirs, x_in.at[q, d - 1], xs[d - 1], sem(2, q), sem(2, q), 32)
        elif step == 3:
            arrived(x_in.at[q], sem(2, q))
            rows = at(x * 32, 32)
            total = mine[q, rows] + core_in[q, rows]
            for d in range(3):
                total = total + x_in[q, d].astype(F32)
            sums[q] = total
            zh_out[q] = total.astype(BF16)
            send(zh_out.at[q], zh_in.at[q], partner, sem(3, q), sem(3, q), 32)
        elif step == 4:
            arrived(zh_in.at[q], sem(3, q))
            total = sums[q] + zh_in[q].astype(F32)
            if a == 0:
                hidden[j] = total
                result = gelu(total)
            else:
                result = total * gelu_slope(hidden[j])
            act[a, core, group] = result.astype(BF16)
            theirs = act.at[a, core, group]
            for device in xs:
                send(theirs, theirs, device, sem(5, q), sem(5, q), 32)
        elif step == 6:
            arrived(act.at[a, core, pl.ds(j * 128, 96)], sem(5, q))
            theirs = act.at[a, core, chunk]
            send(theirs, theirs, other_core, sem(6, q), sem(6, q), 128)
        elif step == 7:
            weights(1 - a)

            def term(half):
                block = act[a, half, chunk]
                if a == 0:
                    return contract(block, down[half], 1, 0)
                return contract(block, up[half], 1, 1)

            total = term(core)
            arrived(act.at[a, 1 - core, chunk], sem(6, q))
            total = total + term(1 - core)
            part[q] = total
            y_out[q] = total.astype(BF16)
            for d in (1, 2, 3):
                theirs = y_out.at[q, at((y + d) % 4 * 32, 32)]
                send(theirs, y_in.at[q, d - 1], ys[d - 1], sem(7, q), sem(7, q), 32)
        else:
            arrived(y_in.at[q], sem(7, q))
            total = part[q, at(y * 32, 32)]
            for d in range(3):
                total = total + y_in[q, d].astype(F32)
            if j == 0:
                kept[a] = total
            else:
                z_out[a, j - 1] = total.astype(BF16)
                send(z_out.at[a, j - 1], z_in.at[a, j - 1], zs[j - 1], sem(8, a), sem(8, a), 32)

    for half in range(2):
        grad_down[pl.ds(half * 768, 768)] = contract(act[0, half], tokens[1], 0, 0).astype(BF16)
        grad_up[:, pl.ds(half * 768, 768)] = contract(tokens[0], act[1, half], 0, 0).astype(BF16)

    for a, result in enumerate((outputs, grad_in)):
        arrived(z_in.at[a], sem(8, a))
        total = kept[a]
        for j in range(3):
            total = total + z_in[a, j].astype(F32)
        result[...] = total.astype(BF16)

    for send_sem, rows in flights.items():
        ref = tokens.at[0, pl.ds(0, rows)]
        pltpu.make_async_copy(ref, ref, sent.at[send_sem]).wait()


def write(*refs):
    count = len(refs) // 2
    sem = refs[-1]
    copies = [
        pltpu.make_async_copy(refs[k], refs[count + k], sem.at[k]) for k in range(count)
    ]
    for copy in copies:
        copy.start()
    for copy in copies:
        copy.wait()


def on_device(inputs, w_up, w_down, grad_out):
    shapes = ((32, 768), (32, 768), (768, 1536), (1536, 768))
    hbm, vmem = pl.BlockSpec(memory_space=pltpu.HBM), pl.BlockSpec(memory_space=pltpu.VMEM)
    results = pl.pallas_call(
        kernel,
        out_shape=tuple(pltpu.VMEM(shape, BF16) for shape in shapes),
        in_specs=[hbm] * 4,
        out_specs=(vmem,) * 4,
        scratch_shapes=[
            pltpu.VMEM((2, 512, 768), BF16),
            pltpu.VMEM((2, 768, 768), BF16),
            pltpu.VMEM((2, 768, 768), BF16),
            pltpu.VMEM((2, 2, 512, 768), BF16),
            pltpu.VMEM((8, 128, 768), F32),
            pltpu.VMEM((8, 128, 768), F32),
            pltpu.VMEM((8, 128, 768), F32),
            pltpu.VMEM((8, 128, 768), BF16),
            pltpu.VMEM((8, 3, 32, 768), BF16),
            pltpu.VMEM((8, 32, 768), F32),
            pltpu.VMEM((8, 32, 768), BF16),
            pltpu.VMEM((8, 32, 768), BF16),
            pltpu.VMEM((4, 32, 768), F32),
            pltpu.VMEM((8, 128, 768), F32),
            pltpu.VMEM((8, 128, 768), BF16),
            pltpu.VMEM((8, 3, 32, 768), BF16),
            pltpu.VMEM((2, 32, 768), F32),
            pltpu.VMEM((2, 3, 32, 768), BF16),
            pltpu.VMEM((2, 3, 32, 768), BF16),
            pltpu.SemaphoreType.DMA((2, 2)),
            pltpu.SemaphoreType.DMA((2,)),
            pltpu.SemaphoreType.DMA((80,)),
            pltpu.SemaphoreType.DMA((80,)),
        ],
        compiler_params=pltpu.CompilerParams(
            collective_id=0, has_side_effects=True, vmem_limit_bytes=56 << 20
        ),
    )(inputs, w_up, w_down, grad_out)
    return pl.pallas_call(
        write,
        out_shape=tuple(jax.ShapeDtypeStruct(shape, BF16) for shape in shapes),
        in_specs=[pl.BlockSpec(memory_space=pl.ANY)] * 4,
        out_specs=(hbm,) * 4,
        scratch_shapes=[pltpu.SemaphoreType.DMA((4,))],
        compiler_params=pltpu.CompilerParams(vmem_limit_bytes=1 << 20),
    )(*results)


def solution(mesh):
    placed = (P("col", "row"), P("row", "col"), P("col", "row"), P("col", "row"))
    return jax.shard_map(
        on_device,
        mesh=mesh,
        in_specs=placed,
        out_specs=(P("col", "row"), P("col", "row"), P("row", "col"), P("col", "row")),
        check_vma=False,
    )
```

```python
import functools

import jax
import jax.numpy as jnp
from jax import lax
from jax.experimental import pallas as pl
from jax.experimental.pallas import tpu as pltpu
from jax.sharding import PartitionSpec as P

MESH = pl.DeviceIdType.MESH
BF16, F32 = jnp.bfloat16, jnp.float32
ORDER = (
    (0, 0, 1), (0, 1, 0), (1, 0, 0), (0, 1, 1), (1, 0, 1), (2, 0, 0), (0, 3, 0), (1, 1, 0),
    (0, 2, 0), (2, 0, 1), (1, 1, 1), (0, 3, 1), (2, 1, 0), (1, 3, 0), (0, 2, 1), (2, 1, 1),
    (1, 2, 0), (3, 0, 1), (2, 3, 0), (1, 3, 1), (3, 1, 0), (2, 2, 0), (1, 2, 1), (3, 1, 1),
    (2, 3, 1), (3, 3, 0), (2, 2, 1), (3, 2, 0), (4, 1, 0), (3, 3, 1), (4, 1, 1), (3, 2, 1),
    (4, 3, 0), (4, 2, 0), (6, 1, 0), (3, 0, 0), (4, 3, 1), (6, 1, 1), (7, 1, 0), (4, 2, 1),
    (6, 3, 0), (7, 1, 1), (6, 2, 0), (4, 0, 0), (7, 3, 0), (6, 3, 1), (7, 2, 0), (4, 0, 1),
    (6, 2, 1), (7, 3, 1), (8, 1, 1), (6, 0, 0), (8, 3, 0), (7, 2, 1), (8, 2, 0), (6, 0, 1),
    (7, 0, 0), (8, 3, 1), (8, 1, 0), (7, 0, 1), (8, 2, 1), (9, 0, 0), (9, 1, 0), (9, 1, 1),
    (9, 0, 1), (8, 0, 0), (8, 0, 1),
)


def tanh_of(value):
    return jnp.tanh(0.7978845608 * (value + 0.044715 * value * value * value))


def gelu(value):
    return 0.5 * value * (1.0 + tanh_of(value))


def gelu_slope(value):
    t = tanh_of(value)
    inner_slope = 0.7978845608 * (1.0 + 3.0 * 0.044715 * value * value)
    return 0.5 * (1.0 + t) + 0.5 * value * (1.0 - t * t) * inner_slope


def contract(left, right, left_dim, right_dim):
    return lax.dot_general(
        left, right, (((left_dim,), (right_dim,)), ((), ())), preferred_element_type=F32
    )


def at(start, size):
    return pl.ds(pl.multiple_of(start, size), size)


def kernel(
    inputs, w_up, w_down, grad_out, outputs, grad_in, grad_up, grad_down,
    tokens, up, down, act,
    core_out, core_in, mine, x_out, x_in, sums, zh_out, zh_in, hidden,
    part, y_out, y_in, kept, z_out, z_in,
    load_sem, own_sem, sent, got,
):
    row, col = lax.axis_index("row"), lax.axis_index("col")
    x, zh, core = row // 4, (row // 2) % 2, row % 2
    zl, y = col // 4, col % 4
    other_core = (row + 1 - 2 * core, col)
    partner = (row + 2 - 4 * zh, col)
    xs = [((row + 4 * d) % 16, col) for d in (1, 2, 3)]
    ys = [(row, zl * 4 + (y + d) % 4) for d in (1, 2, 3)]
    planes = [zl, zl + 1 - 2 * (zl % 2), (zl + 2) % 4, 3 - zl]
    zs = [(row, plane * 4 + y) for plane in planes[1:]]
    shards = (inputs, grad_out)

    loads = []
    for half in range(2):
        for k, (src, dst) in enumerate((
            (w_up.at[:, pl.ds(half * 768, 768)], up.at[half]),
            (w_down.at[pl.ds(half * 768, 768)], down.at[half]),
        )):
            loads.append(pltpu.make_async_copy(src, dst, load_sem.at[k, half]))
    own = [
        pltpu.make_async_copy(shards[a], tokens.at[a, at(y * 32, 32)], own_sem.at[a])
        for a in range(2)
    ]
    for copy in own + loads:
        copy.start()

    barrier = pltpu.get_barrier_semaphore()
    everyone = [other_core, partner] + xs + ys + zs
    for device in everyone:
        pl.semaphore_signal(barrier, inc=1, device_id=device, device_id_type=MESH)
    pl.semaphore_wait(barrier, len(everyone))

    for copy in own:
        copy.wait()
    flights = {}

    def send(src, dst, device, send_sem, recv_sem, rows):
        pltpu.make_async_remote_copy(
            src_ref=src, dst_ref=dst, send_sem=sent.at[send_sem], recv_sem=got.at[recv_sem],
            device_id=device, device_id_type=MESH,
        ).start()
        flights[send_sem] = flights.get(send_sem, 0) + rows

    def arrived(ref, recv_sem):
        pltpu.make_async_copy(ref, ref, got.at[recv_sem]).wait()

    def sem(step, q):
        return 8 + 8 * step + q

    def share(a):
        here = tokens.at[a, at(y * 32, 32)]
        for device in ys:
            send(here, here, device, a, a, 32)

    share(0)
    for j, a in ((1, 0), (3, 0), (1, 1), (3, 1), (2, 0), (2, 1)):
        there = tokens.at[a, at(j * 128 + y * 32, 32)]
        send(tokens.at[a, at(y * 32, 32)], there, zs[j - 1], sem(0, 2 * j + a), sem(0, 2 * j + a), 32)

    weights_here = set()

    def weights(k):
        if k not in weights_here:
            weights_here.add(k)
            for half in range(2):
                loads[2 * half + k].wait()

    for step, j, a in ORDER:
        q = 2 * j + a
        chunk = pl.ds(j * 128, 128)
        group = at(j * 128 + x * 32, 32)
        if step == 0 and j == 0:
            share(a)
        elif step == 0:
            shard = tokens.at[a, at(j * 128 + y * 32, 32)]
            arrived(shard, sem(0, q))
            for device in ys:
                send(shard, shard, device, q, q, 32)
        elif step == 1:
            weights(a)
            arrived(tokens.at[a, pl.ds(j * 128, 96)], q)
            block = tokens[a, chunk]

            def product(half):
                if a == 0:
                    return contract(block, up[half], 1, 0)
                return contract(block, down[half], 1, 1)

            core_out[q] = product(1 - core)
            send(core_out.at[q], core_in.at[q], other_core, sem(1, q), sem(1, q), 256)
            mine[q] = product(core)
        elif step == 2:
            arrived(core_in.at[q], sem(1, q))
            both = mine[q] + core_in[q]
            x_out[q] = both.astype(BF16)
            for d in (1, 2, 3):
                theirs = x_out.at[q, at((x + d) % 4 * 32, 32)]
                send(theirs, x_in.at[q, d - 1], xs[d - 1], sem(2, q), sem(2, q), 32)
        elif step == 3:
            arrived(x_in.at[q], sem(2, q))
            rows = at(x * 32, 32)
            total = mine[q, rows] + core_in[q, rows]
            for d in range(3):
                total = total + x_in[q, d].astype(F32)
            sums[q] = total
            zh_out[q] = total.astype(BF16)
            send(zh_out.at[q], zh_in.at[q], partner, sem(3, q), sem(3, q), 32)
        elif step == 4:
            arrived(zh_in.at[q], sem(3, q))
            total = sums[q] + zh_in[q].astype(F32)
            if a == 0:
                hidden[j] = total
                result = gelu(total)
            else:
                result = total * gelu_slope(hidden[j])
            act[a, core, group] = result.astype(BF16)
            theirs = act.at[a, core, group]
            for device in xs:
                send(theirs, theirs, device, sem(5, q), sem(5, q), 32)
        elif step == 6:
            arrived(act.at[a, core, pl.ds(j * 128, 96)], sem(5, q))
            theirs = act.at[a, core, chunk]
            send(theirs, theirs, other_core, sem(6, q), sem(6, q), 128)
        elif step == 7:
            weights(1 - a)

            def term(half):
                block = act[a, half, chunk]
                if a == 0:
                    return contract(block, down[half], 1, 0)
                return contract(block, up[half], 1, 1)

            total = term(core)
            arrived(act.at[a, 1 - core, chunk], sem(6, q))
            total = total + term(1 - core)
            part[q] = total
            y_out[q] = total.astype(BF16)
            for d in (1, 2, 3):
                theirs = y_out.at[q, at((y + d) % 4 * 32, 32)]
                send(theirs, y_in.at[q, d - 1], ys[d - 1], sem(7, q), sem(7, q), 32)
        elif step == 8:
            arrived(y_in.at[q], sem(7, q))
            total = part[q, at(y * 32, 32)]
            for d in range(3):
                total = total + y_in[q, d].astype(F32)
            if j == 0:
                kept[a] = total
            else:
                z_out[a, j - 1] = total.astype(BF16)
                send(z_out.at[a, j - 1], z_in.at[a, j - 1], zs[j - 1], sem(8, a), sem(8, a), 32)
        else:
            half = 1 - core if j else core
            if a == 0:
                product = contract(act[0, half], tokens[1], 0, 0)
                grad_down[at(half * 768, 768)] = product.astype(BF16)
            else:
                product = contract(tokens[0], act[1, half], 0, 0)
                grad_up[:, at(half * 768, 768)] = product.astype(BF16)

    for a, result in enumerate((outputs, grad_in)):
        arrived(z_in.at[a], sem(8, a))
        total = kept[a]
        for j in range(3):
            total = total + z_in[a, j].astype(F32)
        result[...] = total.astype(BF16)

    for send_sem, rows in flights.items():
        ref = tokens.at[0, pl.ds(0, rows)]
        pltpu.make_async_copy(ref, ref, sent.at[send_sem]).wait()


def write(*refs):
    count = len(refs) // 2
    sem = refs[-1]
    copies = [
        pltpu.make_async_copy(refs[k], refs[count + k], sem.at[k]) for k in range(count)
    ]
    for copy in copies:
        copy.start()
    for copy in copies:
        copy.wait()


def on_device(inputs, w_up, w_down, grad_out):
    shapes = ((32, 768), (32, 768), (768, 1536), (1536, 768))
    hbm, vmem = pl.BlockSpec(memory_space=pltpu.HBM), pl.BlockSpec(memory_space=pltpu.VMEM)
    results = pl.pallas_call(
        kernel,
        out_shape=tuple(pltpu.VMEM(shape, BF16) for shape in shapes),
        in_specs=[hbm] * 4,
        out_specs=(vmem,) * 4,
        scratch_shapes=[
            pltpu.VMEM((2, 512, 768), BF16),
            pltpu.VMEM((2, 768, 768), BF16),
            pltpu.VMEM((2, 768, 768), BF16),
            pltpu.VMEM((2, 2, 512, 768), BF16),
            pltpu.VMEM((8, 128, 768), F32),
            pltpu.VMEM((8, 128, 768), F32),
            pltpu.VMEM((8, 128, 768), F32),
            pltpu.VMEM((8, 128, 768), BF16),
            pltpu.VMEM((8, 3, 32, 768), BF16),
            pltpu.VMEM((8, 32, 768), F32),
            pltpu.VMEM((8, 32, 768), BF16),
            pltpu.VMEM((8, 32, 768), BF16),
            pltpu.VMEM((4, 32, 768), F32),
            pltpu.VMEM((8, 128, 768), F32),
            pltpu.VMEM((8, 128, 768), BF16),
            pltpu.VMEM((8, 3, 32, 768), BF16),
            pltpu.VMEM((2, 32, 768), F32),
            pltpu.VMEM((2, 3, 32, 768), BF16),
            pltpu.VMEM((2, 3, 32, 768), BF16),
            pltpu.SemaphoreType.DMA((2, 2)),
            pltpu.SemaphoreType.DMA((2,)),
            pltpu.SemaphoreType.DMA((80,)),
            pltpu.SemaphoreType.DMA((80,)),
        ],
        compiler_params=pltpu.CompilerParams(
            collective_id=0, has_side_effects=True, vmem_limit_bytes=56 << 20
        ),
    )(inputs, w_up, w_down, grad_out)
    return pl.pallas_call(
        write,
        out_shape=tuple(jax.ShapeDtypeStruct(shape, BF16) for shape in shapes),
        in_specs=[pl.BlockSpec(memory_space=pl.ANY)] * 4,
        out_specs=(hbm,) * 4,
        scratch_shapes=[pltpu.SemaphoreType.DMA((4,))],
        compiler_params=pltpu.CompilerParams(vmem_limit_bytes=1 << 20),
    )(*results)


def solution(mesh):
    placed = (P("col", "row"), P("row", "col"), P("col", "row"), P("col", "row"))
    return jax.shard_map(
        on_device,
        mesh=mesh,
        in_specs=placed,
        out_specs=(P("col", "row"), P("col", "row"), P("row", "col"), P("col", "row")),
        check_vma=False,
    )
```

```python
import functools

import jax
import jax.numpy as jnp
from jax import lax
from jax.experimental import pallas as pl
from jax.experimental.pallas import tpu as pltpu
from jax.sharding import PartitionSpec as P

MESH = pl.DeviceIdType.MESH
BF16, F32 = jnp.bfloat16, jnp.float32
ORDER = (
    (0, 0, 1), (0, 1, 0), (1, 0, 0), (0, 1, 1), (1, 0, 1), (2, 0, 0), (0, 3, 0), (1, 1, 0),
    (0, 2, 0), (2, 0, 1), (1, 1, 1), (0, 3, 1), (2, 1, 0), (1, 3, 0), (0, 2, 1), (2, 1, 1),
    (1, 2, 0), (3, 0, 1), (2, 3, 0), (1, 3, 1), (3, 1, 0), (2, 2, 0), (1, 2, 1), (3, 1, 1),
    (2, 3, 1), (3, 3, 0), (2, 2, 1), (3, 2, 0), (4, 1, 0), (3, 3, 1), (4, 1, 1), (3, 2, 1),
    (4, 3, 0), (4, 2, 0), (6, 1, 0), (3, 0, 0), (4, 3, 1), (6, 1, 1), (7, 1, 0), (4, 2, 1),
    (6, 3, 0), (7, 1, 1), (6, 2, 0), (4, 0, 0), (7, 3, 0), (6, 3, 1), (7, 2, 0), (4, 0, 1),
    (6, 2, 1), (7, 3, 1), (8, 1, 1), (6, 0, 0), (8, 3, 0), (7, 2, 1), (8, 2, 0), (6, 0, 1),
    (7, 0, 0), (8, 3, 1), (8, 1, 0), (7, 0, 1), (8, 2, 1), (9, 0, 0), (9, 1, 0), (9, 1, 1),
    (9, 0, 1), (8, 0, 0), (8, 0, 1),
)


def tanh_of(value):
    return jnp.tanh(0.7978845608 * (value + 0.044715 * value * value * value))


def gelu(value):
    return 0.5 * value * (1.0 + tanh_of(value))


def gelu_slope(value):
    t = tanh_of(value)
    inner_slope = 0.7978845608 * (1.0 + 3.0 * 0.044715 * value * value)
    return 0.5 * (1.0 + t) + 0.5 * value * (1.0 - t * t) * inner_slope


def contract(left, right, left_dim, right_dim):
    return lax.dot_general(
        left, right, (((left_dim,), (right_dim,)), ((), ())), preferred_element_type=F32
    )


def at(start, size):
    return pl.ds(pl.multiple_of(start, size), size)


def kernel(
    inputs, w_up, w_down, grad_out, outputs, grad_in, grad_up, grad_down,
    tokens, up, down, act,
    core_out, core_in, mine, x_out, x_in, sums, zh_out, zh_in, hidden,
    part, y_out, y_in, kept, z_out, z_in,
    load_sem, own_sem, sent, got,
):
    row, col = lax.axis_index("row"), lax.axis_index("col")
    x, zh, core = row // 4, (row // 2) % 2, row % 2
    zl, y = col // 4, col % 4
    other_core = (row + 1 - 2 * core, col)
    partner = (row + 2 - 4 * zh, col)
    xs = [((row + 4 * d) % 16, col) for d in (1, 2, 3)]
    ys = [(row, zl * 4 + (y + d) % 4) for d in (1, 2, 3)]
    planes = [zl, zl + 1 - 2 * (zl % 2), (zl + 2) % 4, 3 - zl]
    zs = [(row, plane * 4 + y) for plane in planes[1:]]
    shards = (inputs, grad_out)

    barrier = pltpu.get_barrier_semaphore()
    everyone = [other_core, partner] + xs + ys + zs
    for device in everyone:
        pl.semaphore_signal(barrier, inc=1, device_id=device, device_id_type=MESH)

    loads = []
    for half in range(2):
        for k, (src, dst) in enumerate((
            (w_up.at[:, pl.ds(half * 768, 768)], up.at[half]),
            (w_down.at[pl.ds(half * 768, 768)], down.at[half]),
        )):
            loads.append(pltpu.make_async_copy(src, dst, load_sem.at[k, half]))
    own = [
        pltpu.make_async_copy(shards[a], tokens.at[a, at(y * 32, 32)], own_sem.at[a])
        for a in range(2)
    ]
    for copy in own + loads:
        copy.start()

    pl.semaphore_wait(barrier, len(everyone))

    for copy in own:
        copy.wait()
    flights = {}

    def send(src, dst, device, send_sem, recv_sem, rows):
        pltpu.make_async_remote_copy(
            src_ref=src, dst_ref=dst, send_sem=sent.at[send_sem], recv_sem=got.at[recv_sem],
            device_id=device, device_id_type=MESH,
        ).start()
        flights[send_sem] = flights.get(send_sem, 0) + rows

    def arrived(ref, recv_sem):
        pltpu.make_async_copy(ref, ref, got.at[recv_sem]).wait()

    def sem(step, q):
        return 8 + 8 * step + q

    def share(a):
        here = tokens.at[a, at(y * 32, 32)]
        for device in ys:
            send(here, here, device, a, a, 32)

    share(0)
    for j, a in ((1, 0), (3, 0), (1, 1), (3, 1), (2, 0), (2, 1)):
        there = tokens.at[a, at(j * 128 + y * 32, 32)]
        send(tokens.at[a, at(y * 32, 32)], there, zs[j - 1], sem(0, 2 * j + a), sem(0, 2 * j + a), 32)

    weights_here = set()

    def weights(k):
        if k not in weights_here:
            weights_here.add(k)
            for half in range(2):
                loads[2 * half + k].wait()

    for step, j, a in ORDER:
        q = 2 * j + a
        chunk = pl.ds(j * 128, 128)
        group = at(j * 128 + x * 32, 32)
        if step == 0 and j == 0:
            share(a)
        elif step == 0:
            shard = tokens.at[a, at(j * 128 + y * 32, 32)]
            arrived(shard, sem(0, q))
            for device in ys:
                send(shard, shard, device, q, q, 32)
        elif step == 1:
            weights(a)
            arrived(tokens.at[a, pl.ds(j * 128, 96)], q)
            block = tokens[a, chunk]

            def product(half):
                if a == 0:
                    return contract(block, up[half], 1, 0)
                return contract(block, down[half], 1, 1)

            core_out[q] = product(1 - core)
            send(core_out.at[q], core_in.at[q], other_core, sem(1, q), sem(1, q), 256)
            mine[q] = product(core)
        elif step == 2:
            arrived(core_in.at[q], sem(1, q))
            both = mine[q] + core_in[q]
            x_out[q] = both.astype(BF16)
            for d in (2, 1, 3):
                theirs = x_out.at[q, at((x + d) % 4 * 32, 32)]
                send(theirs, x_in.at[q, d - 1], xs[d - 1], sem(2, q), sem(2, q), 32)
        elif step == 3:
            arrived(x_in.at[q], sem(2, q))
            rows = at(x * 32, 32)
            total = mine[q, rows] + core_in[q, rows]
            for d in range(3):
                total = total + x_in[q, d].astype(F32)
            sums[q] = total
            zh_out[q] = total.astype(BF16)
            send(zh_out.at[q], zh_in.at[q], partner, sem(3, q), sem(3, q), 32)
        elif step == 4:
            arrived(zh_in.at[q], sem(3, q))
            total = sums[q] + zh_in[q].astype(F32)
            if a == 0:
                hidden[j] = total
                result = gelu(total)
            else:
                result = total * gelu_slope(hidden[j])
            act[a, core, group] = result.astype(BF16)
            theirs = act.at[a, core, group]
            for device in xs:
                send(theirs, theirs, device, sem(5, q), sem(5, q), 32)
        elif step == 6:
            arrived(act.at[a, core, pl.ds(j * 128, 96)], sem(5, q))
            theirs = act.at[a, core, chunk]
            send(theirs, theirs, other_core, sem(6, q), sem(6, q), 128)
        elif step == 7:
            weights(1 - a)

            def term(half):
                block = act[a, half, chunk]
                if a == 0:
                    return contract(block, down[half], 1, 0)
                return contract(block, up[half], 1, 1)

            total = term(core)
            arrived(act.at[a, 1 - core, chunk], sem(6, q))
            total = total + term(1 - core)
            part[q] = total
            y_out[q] = total.astype(BF16)
            for d in (2, 1, 3):
                theirs = y_out.at[q, at((y + d) % 4 * 32, 32)]
                send(theirs, y_in.at[q, d - 1], ys[d - 1], sem(7, q), sem(7, q), 32)
        elif step == 8:
            arrived(y_in.at[q], sem(7, q))
            total = part[q, at(y * 32, 32)]
            for d in range(3):
                total = total + y_in[q, d].astype(F32)
            if j == 0:
                kept[a] = total
            else:
                z_out[a, j - 1] = total.astype(BF16)
                send(z_out.at[a, j - 1], z_in.at[a, j - 1], zs[j - 1], sem(8, a), sem(8, a), 32)
        else:
            half = 1 - core if j else core
            if a == 0:
                product = contract(act[0, half], tokens[1], 0, 0)
                grad_down[at(half * 768, 768)] = product.astype(BF16)
            else:
                product = contract(tokens[0], act[1, half], 0, 0)
                grad_up[:, at(half * 768, 768)] = product.astype(BF16)

    for a, result in enumerate((outputs, grad_in)):
        arrived(z_in.at[a], sem(8, a))
        total = kept[a]
        for j in range(3):
            total = total + z_in[a, j].astype(F32)
        result[...] = total.astype(BF16)

    for send_sem, rows in flights.items():
        ref = tokens.at[0, pl.ds(0, rows)]
        pltpu.make_async_copy(ref, ref, sent.at[send_sem]).wait()


def write(*refs):
    count = len(refs) // 2
    sem = refs[-1]
    copies = [
        pltpu.make_async_copy(refs[k], refs[count + k], sem.at[k]) for k in range(count)
    ]
    for copy in copies:
        copy.start()
    for copy in copies:
        copy.wait()


def on_device(inputs, w_up, w_down, grad_out):
    shapes = ((32, 768), (32, 768), (768, 1536), (1536, 768))
    hbm, vmem = pl.BlockSpec(memory_space=pltpu.HBM), pl.BlockSpec(memory_space=pltpu.VMEM)
    results = pl.pallas_call(
        kernel,
        out_shape=tuple(pltpu.VMEM(shape, BF16) for shape in shapes),
        in_specs=[hbm] * 4,
        out_specs=(vmem,) * 4,
        scratch_shapes=[
            pltpu.VMEM((2, 512, 768), BF16),
            pltpu.VMEM((2, 768, 768), BF16),
            pltpu.VMEM((2, 768, 768), BF16),
            pltpu.VMEM((2, 2, 512, 768), BF16),
            pltpu.VMEM((8, 128, 768), F32),
            pltpu.VMEM((8, 128, 768), F32),
            pltpu.VMEM((8, 128, 768), F32),
            pltpu.VMEM((8, 128, 768), BF16),
            pltpu.VMEM((8, 3, 32, 768), BF16),
            pltpu.VMEM((8, 32, 768), F32),
            pltpu.VMEM((8, 32, 768), BF16),
            pltpu.VMEM((8, 32, 768), BF16),
            pltpu.VMEM((4, 32, 768), F32),
            pltpu.VMEM((8, 128, 768), F32),
            pltpu.VMEM((8, 128, 768), BF16),
            pltpu.VMEM((8, 3, 32, 768), BF16),
            pltpu.VMEM((2, 32, 768), F32),
            pltpu.VMEM((2, 3, 32, 768), BF16),
            pltpu.VMEM((2, 3, 32, 768), BF16),
            pltpu.SemaphoreType.DMA((2, 2)),
            pltpu.SemaphoreType.DMA((2,)),
            pltpu.SemaphoreType.DMA((80,)),
            pltpu.SemaphoreType.DMA((80,)),
        ],
        compiler_params=pltpu.CompilerParams(
            collective_id=0, has_side_effects=True, vmem_limit_bytes=56 << 20
        ),
    )(inputs, w_up, w_down, grad_out)
    return pl.pallas_call(
        write,
        out_shape=tuple(jax.ShapeDtypeStruct(shape, BF16) for shape in shapes),
        in_specs=[pl.BlockSpec(memory_space=pl.ANY)] * 4,
        out_specs=(hbm,) * 4,
        scratch_shapes=[pltpu.SemaphoreType.DMA((4,))],
        compiler_params=pltpu.CompilerParams(vmem_limit_bytes=1 << 20),
    )(*results)


def solution(mesh):
    placed = (P("col", "row"), P("row", "col"), P("col", "row"), P("col", "row"))
    return jax.shard_map(
        on_device,
        mesh=mesh,
        in_specs=placed,
        out_specs=(P("col", "row"), P("col", "row"), P("row", "col"), P("col", "row")),
        check_vma=False,
    )
```
